32 devices in a mesh: grp: 2 (over y), slab: 4 (over z), exp: 2 (over x), sub: 2 (over core).
Axes of the slice: x: 2, y: 2, z: 4, core: 2. Of those that a mesh axis runs over, the one named last changes fastest.
Arguments:
- start_u: float32 [4, 16, 256, 256], P(('grp', 'exp'), 'slab', 'sub'), parts along dimension 0, may hold values from 0.2 to 1
- start_v: float32 [4, 16, 256, 256], P(('grp', 'exp'), 'slab', 'sub'), parts along dimension 0, may hold values from 0 to 0.5
- feed: float32 [32, 256, 256], P(('grp', 'slab'), 'sub'), parts along dimension 0, may hold values from 0.02 to 0.2
- labels: int32 [4, 256, 256], P(('grp', 'exp'), 'sub'), parts along dimension 0, may hold values from 0 to 3
- direction: float32 [32, 256, 256], P(('grp', 'slab'), ('sub', 'exp')), parts along dimension 0, may hold values from -6 to 6
Outputs:
- hess_vec: float32 [32, 256, 256], P(('grp', 'slab'), ('sub', 'exp')), parts along dimension 0
The draws below stay inside these ranges and needn't reach their ends.
There are 2 independent parts, one for each index of `grp`. The reference program is written for one: setup_inputs(seed, part) draws one part's arguments, and reference() takes and returns one part's arrays. A program takes and returns all parts, laid end to end along the dimension named above; each array names one. Nothing has to cross between parts.
All inputs are finite; a program needn't handle non-finite values.
Results may differ from the reference program's by a relative error of at most 0.00002.
Values sent between devices are 32-bit elements; how exact they have to be, the bound alone decides.
A program may use at most 64 MiB of HBM per device.

```python
import math
import jax
import jax.numpy as jnp

NX = 256
STEPS = 3
E = 2
NY = 256
NZ = 16


def touch_ends(entries, rng, low, largest):
    longest = entries.shape.index(max(entries.shape))
    spots = []
    for shift in (0, 1):
        where = [jax.random.randint(jax.random.fold_in(rng, axis), (), 0, length) for axis, length in enumerate(entries.shape)]
        where[longest] = (where[longest] + shift) % entries.shape[longest]
        spots.append(tuple(where))
    return entries.at[spots[0]].set(low).at[spots[1]].set(largest)


def steps_of(rng, dims, cuts, low, largest):
    gain, own = 1.0, jax.random.fold_in(rng, 6)
    for position, shards_of in cuts:
        heights = jnp.exp(jax.random.uniform(jax.random.fold_in(own, position), (shards_of,), jnp.float32, low / len(cuts), largest / len(cuts)))
        gain = gain * jnp.repeat(heights, dims[position] // shards_of).reshape([-1 if axis == position else 1 for axis in range(len(dims))])
    return gain


def centred(rng, dims, width, limit, cuts=(), kind=jnp.bfloat16):
    entries = jax.random.normal(rng, dims, jnp.float32) * width
    if len(cuts) > 0:
        entries = steps_of(rng, dims, cuts, -0.22, 0.18) * entries
    return jnp.clip(entries, min=-limit, max=limit).astype(kind)


def setup_inputs(seed: int = 0, part: int = 0) -> dict:
    key_of = jax.random.split(jax.random.key(seed), 6)
    part_splits = jax.random.split(jax.random.fold_in(key_of[5], part), 6)
    start_u = jnp.clip(0.2 + 0.8 * jax.random.uniform(part_splits[0], (E, NZ, NY, NX), jnp.float32) ** steps_of(part_splits[0], (E, NZ, NY, NX), ((0, 2), (1, 4), (2, 2)), -0.2, 0.2), 0.2, 1.0)
    start_v = jnp.clip(0.5 * jax.random.uniform(part_splits[1], (E, NZ, NY, NX), jnp.float32) ** steps_of(part_splits[1], (E, NZ, NY, NX), ((0, 2), (1, 4), (2, 2)), -0.2, 0.2), 0.0, 0.5)
    feed = jnp.clip(jnp.exp(math.log(0.2) - 2.3025851 * jax.random.uniform(part_splits[2], (NZ, NY, NX), jnp.float32) ** steps_of(part_splits[2], (NZ, NY, NX), ((0, 4), (1, 2)), -0.2, 0.2)), 0.02, 0.2)
    labels = touch_ends(jax.random.randint(part_splits[3], (E, NY, NX), 0, 4), jax.random.fold_in(part_splits[3], 1), 0, 3).astype(jnp.int32)
    direction = centred(part_splits[4], (NZ, NY, NX), 1.0, 6.0, ((0, 4), (1, 4)), jnp.float32)
    return dict(start_u=start_u, start_v=start_v, feed=feed, labels=labels, direction=direction)


diff_u = 0.15
diff_v = 0.075
kill = 0.06


def laplace(field):
    padded = jnp.pad(field, ((0, 0), (1, 1), (1, 1), (1, 1)))
    total = padded[:, 2:, 1:-1, 1:-1] + padded[:, :-2, 1:-1, 1:-1]
    total = total + padded[:, 1:-1, 2:, 1:-1] + padded[:, 1:-1, :-2, 1:-1]
    total = total + padded[:, 1:-1, 1:-1, 2:] + padded[:, 1:-1, 1:-1, :-2]
    return total - 6.0 * field


def reference(start_u, start_v, feed, labels, direction):
    supply = (0.1 * labels.astype(jnp.float32))[:, None]
    rate = feed[None]
    shift = direction[None]
    conc_u, conc_v = start_u, start_v
    tan_u = jnp.zeros_like(start_u)
    tan_v = jnp.zeros_like(start_v)
    states = []
    for step in range(STEPS):
        states.append((conc_u, conc_v))
        both = conc_u * conc_v
        next_tu = tan_u + diff_u * laplace(tan_u) - (conc_v * conc_v + rate) * tan_u - 2.0 * both * tan_v + (1.0 - conc_u) * shift
        next_tv = tan_v + diff_v * laplace(tan_v) + conc_v * conc_v * tan_u + (2.0 * both - rate - kill) * tan_v - conc_v * shift
        if step + 1 < STEPS:
            new_u = conc_u + diff_u * laplace(conc_u) - both * conc_v + rate * (1.0 - conc_u) + supply
            new_v = conc_v + diff_v * laplace(conc_v) + both * conc_v - (rate + kill) * conc_v
            conc_u, conc_v = new_u, new_v
        tan_u, tan_v = next_tu, next_tv
    adj_a, adj_b = tan_u, tan_v
    grad = jnp.zeros_like(start_u)
    for step in reversed(range(STEPS)):
        conc_u, conc_v = states[step]
        grad = grad + (1.0 - conc_u) * adj_a - conc_v * adj_b
        if step > 0:
            both = conc_u * conc_v
            new_a = adj_a + diff_u * laplace(adj_a) - (conc_v * conc_v + rate) * adj_a + conc_v * conc_v * adj_b
            new_b = adj_b + diff_v * laplace(adj_b) - 2.0 * both * adj_a + (2.0 * both - rate - kill) * adj_b
            adj_a, adj_b = new_a, new_b
    return jnp.sum(grad, axis=0)
```

```python
import functools

import jax
import jax.numpy as jnp
from jax import lax
from jax.experimental import pallas as pl
from jax.experimental.pallas import tpu as pltpu
from jax.sharding import PartitionSpec as P

diff_u = 0.15
diff_v = 0.075
kill = 0.06

EDGE = 8
PAD = 8
CHUNK = 32
LO, HI = 2, 5
MESH = pl.DeviceIdType.MESH


def kernel(
    slabs, exps,
    u_in, v_in, feed_in, lab_in, dir_in, out,
    U0, V0, D, F, LAB, U1, V1, U2, V2, P1, Q1, P2, Q2, A3, B3, A2, B2,
    C, CN, G, R, send, recv, local,
):
    own, width = u_in.shape[1], u_in.shape[2]
    rows = own + EDGE
    part = own // exps
    grp, slab = lax.axis_index("grp"), lax.axis_index("slab")
    exp, sub = lax.axis_index("exp"), lax.axis_index("sub")
    has = (slab > 0, slab < slabs - 1)
    mate = 1 - sub

    def row(value):
        return pl.multiple_of(value, 8)

    start = row(PAD + EDGE * sub)
    edge_in = row((own - EDGE) * (1 - sub))
    edge_out = row(PAD + own * sub)
    mine = row(start + part * exp)

    def peer(side=None, step=0, other=False):
        z = slab if side is None else slab + (2 * side - 1)
        return (grp, z, lax.rem(exp + step, exps), mate if other else sub)

    count = [0]
    pending = []

    def remote(src, dst, target, sends=None, gets=None):
        i = count[0]
        count[0] += 1
        copy = pltpu.make_async_remote_copy(
            src_ref=src, dst_ref=dst, send_sem=send.at[i], recv_sem=recv.at[i],
            device_id=target, device_id_type=MESH,
        )
        if sends is None:
            copy.start()
        else:
            pl.when(sends)(copy.start)
        pending.append((sends, copy))

        def arrived():
            if gets is None:
                copy.wait_recv()
            else:
                pl.when(gets)(copy.wait_recv)

        return arrived

    loads = []
    for i, (src, dst) in enumerate([
        (u_in, U0.at[LO : HI + 1, pl.ds(start, own)]),
        (v_in, V0.at[LO : HI + 1, pl.ds(start, own)]),
        (feed_in, F.at[LO : HI + 1, pl.ds(start, own)]),
        (lab_in, LAB.at[pl.ds(start, own)]),
        (dir_in, D.at[LO : HI + 1, pl.ds(mine, part)]),
    ]):
        copy = pltpu.make_async_copy(src, dst, local.at[i])
        copy.start()
        loads.append(copy)

    barrier = pltpu.get_barrier_semaphore()

    def greet(target):
        pl.semaphore_signal(barrier, inc=1, device_id=target, device_id_type=MESH)

    greet(peer(other=True))
    for step in range(1, exps):
        greet(peer(step=step))
    for side in (0, 1):
        @pl.when(has[side])
        def _():
            greet(peer(side))
            greet(peer(side, other=True))

    for ref in (U0, V0, U1, V1, P1, Q1, P2, Q2, A3, B3, A2, B2):
        blank = jnp.zeros((ref.shape[0], PAD, width), jnp.float32)
        ref[:, :PAD, :] = blank
        ref[:, PAD + rows :, :] = blank
    for ref in (A2, B2):
        for p in (LO - 1, HI + 1):
            ref[p] = jnp.zeros(ref.shape[1:], jnp.float32)
    for side in (0, 1):
        @pl.when(jnp.logical_not(has[side]))
        def _():
            for ref in (U0, V0, D):
                for p in ((0, 1), (6, 7))[side]:
                    ref[p] = jnp.zeros(ref.shape[1:], jnp.float32)
            for ref in (F, A3, B3):
                ref[(1, 6)[side]] = jnp.zeros(ref.shape[1:], jnp.float32)
            CN[side] = jnp.zeros(CN.shape[1:], jnp.float32)

    near = jnp.where(has[0], 1, 0) + jnp.where(has[1], 1, 0)
    pl.semaphore_wait(barrier, exps + 2 * near)

    outer = (0, 3)
    second = (1, 2)
    first_in = (6, 1)
    second_in = (7, 0)
    pair = ((0, 2), (2, 4))
    pair_in = ((6, 8), (0, 2))

    got_dir, got_feed, got_one, got_two = [], [], [], []
    for side in (0, 1):
        a, b = pair[side]
        c, d = pair_in[side]
        got_dir.append(remote(
            dir_in.at[a:b], D.at[c:d, pl.ds(mine, part)], peer(side), has[side], has[1 - side]))
        got_feed.append(remote(
            feed_in.at[outer[side], pl.ds(row(part * exp), part)],
            F.at[first_in[side], pl.ds(mine, part)], peer(side), has[side], has[1 - side]))
    got_mate = []
    for src, dst in ((u_in, U0), (v_in, V0), (feed_in, F)):
        got_mate.append(remote(
            src.at[:, pl.ds(edge_in, EDGE)], dst.at[LO : HI + 1, pl.ds(edge_out, EDGE)],
            peer(other=True)))
    got_mate.append(remote(
        lab_in.at[pl.ds(edge_in, EDGE)], LAB.at[pl.ds(edge_out, EDGE)], peer(other=True)))
    got_rows = [
        remote(dir_in, D.at[LO : HI + 1, pl.ds(mine, part)], peer(step=step))
        for step in range(1, exps)
    ]
    for side in (0, 1):
        for src, dst in ((u_in, U0), (v_in, V0)):
            got_one.append(remote(
                src.at[outer[side]], dst.at[first_in[side], pl.ds(start, own)],
                peer(side), has[side], has[1 - side]))
    for side in (0, 1):
        a, b = pair[side]
        c, d = pair_in[side]
        for src, dst in ((u_in, U0), (v_in, V0)):
            got_one.append(remote(
                src.at[a:b, pl.ds(edge_in, EDGE)], dst.at[c:d, pl.ds(edge_out, EDGE)],
                peer(side, other=True), has[side], has[1 - side]))
    for side in (0, 1):
        for src, dst in ((u_in, U0), (v_in, V0)):
            got_two.append(remote(
                src.at[second[side]], dst.at[second_in[side], pl.ds(start, own)],
                peer(side), has[side], has[1 - side]))

    def sweep(planes, body, first=PAD, length=rows):
        begin, stride, number = planes

        def plane(i, carry):
            p = begin + stride * i

            def block(j, inner):
                body(p, row(first + j * CHUNK), CHUNK)
                return inner

            lax.fori_loop(0, length // CHUNK, block, 0)
            if length % CHUNK:
                body(p, row(first + length // CHUNK * CHUNK), length % CHUNK)
            return carry

        lax.fori_loop(0, number, plane, 0)

    def held(ref, p, r, n):
        return ref[p, pl.ds(r, n), :]

    def lap(ref, p, r, n):
        core = held(ref, p, r, n)
        wide = ref[p, pl.ds(row(r - 8), n + 16), :]
        lane = lax.broadcasted_iota(jnp.int32, core.shape, 1)
        total = held(ref, p + 1, r, n) + held(ref, p - 1, r, n)
        total = total + wide[9 : 9 + n] + wide[7 : 7 + n]
        total = total + jnp.where(lane == width - 1, 0.0, pltpu.roll(core, width - 1, 1))
        total = total + jnp.where(lane == 0, 0.0, pltpu.roll(core, 1, 1))
        return core, total - 6.0 * core

    def halo_mask(p):
        there = jnp.where(p < LO, has[0], jnp.where(p > HI, has[1], True))
        return jnp.where(there, 1.0, 0.0)

    def forward(src_u, src_v, dst_u, dst_v, halo):
        def body(p, r, n):
            u, lap_u = lap(src_u, p, r, n)
            v, lap_v = lap(src_v, p, r, n)
            rate = held(F, p, r, n)
            react = u * v * v
            supply = 0.1 * LAB[pl.ds(r, n), :].astype(jnp.float32)
            new_u = u + diff_u * lap_u - react + rate * (1.0 - u) + supply
            new_v = v + diff_v * lap_v + react - (rate + kill) * v
            if halo:
                keep = halo_mask(p)
                new_u, new_v = new_u * keep, new_v * keep
            dst_u[p, pl.ds(r, n), :] = new_u
            dst_v[p, pl.ds(r, n), :] = new_v

        return body

    def first_tangent(p, r, n):
        shift = held(D, p, r, n)
        P1[p, pl.ds(r, n), :] = (1.0 - held(U0, p, r, n)) * shift
        Q1[p, pl.ds(r, n), :] = -held(V0, p, r, n) * shift

    def tangent(src_p, src_q, dst_p, dst_q, at_u, at_v, halo):
        def body(p, r, n):
            tan_p, lap_p = lap(src_p, p, r, n)
            tan_q, lap_q = lap(src_q, p, r, n)
            u, v = held(at_u, p, r, n), held(at_v, p, r, n)
            rate, shift = held(F, p, r, n), held(D, p, r, n)
            sq = v * v
            both = 2.0 * (u * v)
            new_p = tan_p + diff_u * lap_p - (sq + rate) * tan_p - both * tan_q + (1.0 - u) * shift
            new_q = tan_q + diff_v * lap_q + sq * tan_p + (both - rate - kill) * tan_q - v * shift
            if halo:
                keep = halo_mask(p)
                new_p, new_q = new_p * keep, new_q * keep
            dst_p[p, pl.ds(r, n), :] = new_p
            dst_q[p, pl.ds(r, n), :] = new_q

        return body

    def adjoint(src_a, src_b, at_u, at_v, p, r, n):
        a, lap_a = lap(src_a, p, r, n)
        b, lap_b = lap(src_b, p, r, n)
        u, v = held(at_u, p, r, n), held(at_v, p, r, n)
        rate = held(F, p, r, n)
        sq = v * v
        both = 2.0 * (u * v)
        new_a = a + diff_u * lap_a - (sq + rate) * a + sq * b
        new_b = b + diff_v * lap_b - both * a + (both - rate - kill) * b
        return a, b, u, v, new_a, new_b

    def second_adjoint(p, r, n):
        new_a, new_b = adjoint(A3, B3, U2, V2, p, r, n)[4:]
        A2[p, pl.ds(r, n), :] = new_a
        B2[p, pl.ds(r, n), :] = new_b

    def product(p, r, n):
        a, b, u, v, new_a, new_b = adjoint(A2, B2, U1, V1, p, r, n)
        total = (1.0 - held(U2, p, r, n)) * held(A3, p, r, n) - held(V2, p, r, n) * held(B3, p, r, n)
        total = total + (1.0 - u) * a - v * b
        total = total + (1.0 - held(U0, p, r, n)) * new_a - held(V0, p, r, n) * new_b
        G[p - LO, pl.ds(row(r - start), n), :] = total

    inner, ends, halos = (3, 1, 2), (2, 3, 2), (1, 5, 2)
    for copy in loads:
        copy.wait()
    for arrived in got_mate:
        arrived()
    sweep(inner, forward(U0, V0, U1, V1, False))

    for arrived in got_dir + got_feed:
        arrived()
    passed = []
    for side in (0, 1):
        planes = ((0, 2), (6, 8))[side]
        for step in range(1, exps):
            for ref in (
                D.at[planes[0] : planes[1], pl.ds(mine, part)],
                F.at[(1, 6)[side], pl.ds(mine, part)],
            ):
                passed.append(remote(ref, ref, peer(step=step), has[side], has[side]))
    for arrived in got_rows + passed:
        arrived()
    mate_row = row(start + edge_in)
    got_edges = [remote(
        D.at[:, pl.ds(mate_row, EDGE)], D.at[:, pl.ds(edge_out, EDGE)], peer(other=True))]
    for p in (1, 6):
        got_edges.append(remote(
            F.at[p, pl.ds(mate_row, EDGE)], F.at[p, pl.ds(edge_out, EDGE)], peer(other=True)))

    for arrived in got_one:
        arrived()
    sweep(ends, forward(U0, V0, U1, V1, False))
    sweep(inner, forward(U1, V1, U2, V2, False))
    for arrived in got_edges:
        arrived()
    sweep((1, 1, 6), first_tangent)
    sweep((2, 1, 4), tangent(P1, Q1, P2, Q2, U1, V1, False))
    sweep(inner, tangent(P2, Q2, A3, B3, U2, V2, False))

    for arrived in got_two:
        arrived()
    sweep((0, 7, 2), first_tangent)
    sweep(halos, forward(U0, V0, U1, V1, True))
    sweep(halos, tangent(P1, Q1, P2, Q2, U1, V1, True))
    sweep(ends, forward(U1, V1, U2, V2, False))
    sweep(ends, tangent(P2, Q2, A3, B3, U2, V2, False))
    got_adj = []
    for side in (0, 1):
        for ref in (A3, B3):
            got_adj.append(remote(
                ref.at[(LO, HI)[side], pl.ds(PAD, rows)],
                ref.at[first_in[side], pl.ds(PAD, rows)],
                peer(side), has[side], has[1 - side]))
    sweep(inner, second_adjoint)
    for arrived in got_adj:
        arrived()
    sweep(ends, second_adjoint)

    got_add = []
    for side in (0, 1):
        p, q = (LO, HI)[side], (1, 6)[side]

        def block(j, carry):
            r = row(start + j * CHUNK)
            C[side, pl.ds(row(j * CHUNK), CHUNK), :] = (
                (1.0 - held(U0, q, r, CHUNK)) * (diff_u * held(A2, p, r, CHUNK))
                - held(V0, q, r, CHUNK) * (diff_v * held(B2, p, r, CHUNK))
            )
            return carry

        lax.fori_loop(0, own // CHUNK, block, 0)
        got_add.append(remote(C.at[side], CN.at[1 - side], peer(side), has[side], has[1 - side]))

    def scatter(which):
        sent = []
        for step in range(1, exps):
            theirs = row(part * lax.rem(exp + step, exps))
            for p in which:
                sent.append(remote(
                    G.at[p, pl.ds(theirs, part)], R.at[step - 1, p], peer(step=step)))
        return sent

    sweep(inner, product, start, own)
    got_sum = scatter((1, 2))
    sweep(ends, product, start, own)
    for arrived in got_add:
        arrived()
    for side in (0, 1):
        def block(j, carry):
            r = pl.ds(row(j * CHUNK), CHUNK)
            G[(0, 3)[side], r, :] += CN[side, r, :]
            return carry

        lax.fori_loop(0, own // CHUNK, block, 0)
    got_sum += scatter((0, 3))
    for arrived in got_sum:
        arrived()
    kept = row(part * exp)
    for p in range(4):
        total = G[p, pl.ds(kept, part), :]
        for step in range(1, exps):
            total = total + R[step - 1, p]
        out[p] = total
    for sends, copy in pending:
        if sends is None:
            copy.wait_send()
        else:
            pl.when(sends)(copy.wait_send)


def solution(mesh):
    slabs, exps = mesh.shape["slab"], mesh.shape["exp"]

    def per_device(start_u, start_v, feed, labels, direction):
        planes, own, width = feed.shape
        part = own // exps
        tall = own + EDGE + 2 * PAD

        def field(*shape):
            return pltpu.VMEM(shape, jnp.float32)

        copies = 64 + 20 * exps
        return pl.pallas_call(
            functools.partial(kernel, slabs, exps),
            out_shape=jax.ShapeDtypeStruct((planes, part, width), jnp.float32),
            in_specs=[pl.BlockSpec(memory_space=pl.ANY)] * 5,
            out_specs=pl.BlockSpec(memory_space=pltpu.VMEM),
            scratch_shapes=(
                [field(8, tall, width)] * 4
                + [pltpu.VMEM((tall, width), jnp.int32)]
                + [field(8, tall, width)] * 12
                + [
                    field(2, own, width),
                    field(2, own, width),
                    field(planes, own, width),
                    field(exps - 1, planes, part, width),
                    pltpu.SemaphoreType.DMA((copies,)),
                    pltpu.SemaphoreType.DMA((copies,)),
                    pltpu.SemaphoreType.DMA((5,)),
                ]
            ),
            compiler_params=pltpu.CompilerParams(
                collective_id=0, has_side_effects=True, vmem_limit_bytes=48 * 1024 * 1024
            ),
        )(start_u[0], start_v[0], feed, labels[0], direction)

    placed = (
        P(("grp", "exp"), "slab", "sub", None),
        P(("grp", "exp"), "slab", "sub", None),
        P(("grp", "slab"), "sub", None),
        P(("grp", "exp"), "sub", None),
        P(("grp", "slab"), ("sub", "exp"), None),
    )
    return jax.shard_map(
        per_device,
        mesh=mesh,
        in_specs=placed,
        out_specs=P(("grp", "slab"), ("sub", "exp"), None),
        check_vma=False,
    )
```

```python
import functools

import jax
import jax.numpy as jnp
from jax import lax
from jax.experimental import pallas as pl
from jax.experimental.pallas import tpu as pltpu
from jax.sharding import PartitionSpec as P

diff_u = 0.15
diff_v = 0.075
kill = 0.06

EDGE = 8
PAD = 8
CHUNK = 32
LO, HI = 2, 5
MESH = pl.DeviceIdType.MESH


def kernel(
    slabs, exps,
    u_in, v_in, feed_in, lab_in, dir_in, out,
    U0, V0, D, F, LAB, U1, V1, U2, V2, P1, Q1, P2, Q2, A3, B3, A2, B2,
    C, CN, G, R, send, recv, local,
):
    own, width = u_in.shape[1], u_in.shape[2]
    rows = own + EDGE
    part = own // exps
    grp, slab = lax.axis_index("grp"), lax.axis_index("slab")
    exp, sub = lax.axis_index("exp"), lax.axis_index("sub")
    has = (slab > 0, slab < slabs - 1)
    mate = 1 - sub

    def row(value):
        return pl.multiple_of(value, 8)

    start = row(PAD + EDGE * sub)
    edge_in = row((own - EDGE) * (1 - sub))
    edge_out = row(PAD + own * sub)
    mine = row(start + part * exp)

    def peer(side=None, step=0, other=False):
        z = slab if side is None else slab + (2 * side - 1)
        return (grp, z, lax.rem(exp + step, exps), mate if other else sub)

    count = [0]
    pending = []

    def remote(src, dst, target, sends=None, gets=None):
        i = count[0]
        count[0] += 1
        copy = pltpu.make_async_remote_copy(
            src_ref=src, dst_ref=dst, send_sem=send.at[i], recv_sem=recv.at[i],
            device_id=target, device_id_type=MESH,
        )
        if sends is None:
            copy.start()
        else:
            pl.when(sends)(copy.start)
        pending.append((sends, copy))

        def arrived():
            if gets is None:
                copy.wait_recv()
            else:
                pl.when(gets)(copy.wait_recv)

        return arrived

    loads = []
    for i, (src, dst) in enumerate([
        (u_in, U0.at[LO : HI + 1, pl.ds(start, own)]),
        (v_in, V0.at[LO : HI + 1, pl.ds(start, own)]),
        (feed_in, F.at[LO : HI + 1, pl.ds(start, own)]),
        (lab_in, LAB.at[pl.ds(start, own)]),
        (dir_in, D.at[LO : HI + 1, pl.ds(mine, part)]),
    ]):
        copy = pltpu.make_async_copy(src, dst, local.at[i])
        copy.start()
        loads.append(copy)

    barrier = pltpu.get_barrier_semaphore()

    def greet(target):
        pl.semaphore_signal(barrier, inc=1, device_id=target, device_id_type=MESH)

    greet(peer(other=True))
    for step in range(1, exps):
        greet(peer(step=step))
    for side in (0, 1):
        @pl.when(has[side])
        def _():
            greet(peer(side))
            greet(peer(side, other=True))

    for ref in (U0, V0, U1, V1, P1, Q1, P2, Q2, A3, B3, A2, B2):
        blank = jnp.zeros((ref.shape[0], PAD, width), jnp.float32)
        ref[:, :PAD, :] = blank
        ref[:, PAD + rows :, :] = blank
    for ref in (A2, B2):
        for p in (LO - 1, HI + 1):
            ref[p] = jnp.zeros(ref.shape[1:], jnp.float32)
    for side in (0, 1):
        @pl.when(jnp.logical_not(has[side]))
        def _():
            for ref in (U0, V0, D):
                for p in ((0, 1), (6, 7))[side]:
                    ref[p] = jnp.zeros(ref.shape[1:], jnp.float32)
            for ref in (F, A3, B3):
                ref[(1, 6)[side]] = jnp.zeros(ref.shape[1:], jnp.float32)
            CN[side] = jnp.zeros(CN.shape[1:], jnp.float32)

    near = jnp.where(has[0], 1, 0) + jnp.where(has[1], 1, 0)
    pl.semaphore_wait(barrier, exps + 2 * near)

    outer = (0, 3)
    second = (1, 2)
    first_in = (6, 1)
    second_in = (7, 0)
    pair = ((0, 2), (2, 4))
    pair_in = ((6, 8), (0, 2))

    got_dir, got_feed, got_one, got_two = [], [], [], []
    for side in (0, 1):
        a, b = pair[side]
        c, d = pair_in[side]
        got_dir.append(remote(
            dir_in.at[a:b], D.at[c:d, pl.ds(mine, part)], peer(side), has[side], has[1 - side]))
        got_feed.append(remote(
            feed_in.at[outer[side], pl.ds(row(part * exp), part)],
            F.at[first_in[side], pl.ds(mine, part)], peer(side), has[side], has[1 - side]))
    got_mate = []
    for src, dst in ((u_in, U0), (v_in, V0), (feed_in, F)):
        got_mate.append(remote(
            src.at[:, pl.ds(edge_in, EDGE)], dst.at[LO : HI + 1, pl.ds(edge_out, EDGE)],
            peer(other=True)))
    got_mate.append(remote(
        lab_in.at[pl.ds(edge_in, EDGE)], LAB.at[pl.ds(edge_out, EDGE)], peer(other=True)))
    got_rows = [
        remote(dir_in, D.at[LO : HI + 1, pl.ds(mine, part)], peer(step=step))
        for step in range(1, exps)
    ]
    for side in (0, 1):
        for src, dst in ((u_in, U0), (v_in, V0)):
            got_one.append(remote(
                src.at[outer[side]], dst.at[first_in[side], pl.ds(start, own)],
                peer(side), has[side], has[1 - side]))
    for side in (0, 1):
        a, b = pair[side]
        c, d = pair_in[side]
        for src, dst in ((u_in, U0), (v_in, V0)):
            got_one.append(remote(
                src.at[a:b, pl.ds(edge_in, EDGE)], dst.at[c:d, pl.ds(edge_out, EDGE)],
                peer(side, other=True), has[side], has[1 - side]))
    upward = 2 * exp >= exps
    blocks = own // CHUNK

    def top(k):
        return row(CHUNK * jnp.where(upward, k, blocks - 1 - k))

    for k in range(blocks):
        got = []
        for side in (0, 1):
            for src, dst in ((u_in, U0), (v_in, V0)):
                got.append(remote(
                    src.at[second[side], pl.ds(top(k), CHUNK)],
                    dst.at[second_in[side], pl.ds(row(start + top(k)), CHUNK)],
                    peer(side), has[side], has[1 - side]))
        got_two.append(got)

    def sweep(planes, body, first=PAD, length=rows):
        begin, stride, number = planes

        def plane(i, carry):
            p = begin + stride * i

            def block(j, inner):
                body(p, row(first + j * CHUNK), CHUNK)
                return inner

            lax.fori_loop(0, length // CHUNK, block, 0)
            if length % CHUNK:
                body(p, row(first + length // CHUNK * CHUNK), length % CHUNK)
            return carry

        lax.fori_loop(0, number, plane, 0)

    def held(ref, p, r, n):
        return ref[p, pl.ds(r, n), :]

    def lap(ref, p, r, n):
        core = held(ref, p, r, n)
        wide = ref[p, pl.ds(row(r - 8), n + 16), :]
        lane = lax.broadcasted_iota(jnp.int32, core.shape, 1)
        total = held(ref, p + 1, r, n) + held(ref, p - 1, r, n)
        total = total + wide[9 : 9 + n] + wide[7 : 7 + n]
        total = total + jnp.where(lane == width - 1, 0.0, pltpu.roll(core, width - 1, 1))
        total = total + jnp.where(lane == 0, 0.0, pltpu.roll(core, 1, 1))
        return core, total - 6.0 * core

    def halo_mask(p):
        there = jnp.where(p < LO, has[0], jnp.where(p > HI, has[1], True))
        return jnp.where(there, 1.0, 0.0)

    def forward(src_u, src_v, dst_u, dst_v, halo):
        def body(p, r, n):
            u, lap_u = lap(src_u, p, r, n)
            v, lap_v = lap(src_v, p, r, n)
            rate = held(F, p, r, n)
            react = u * v * v
            supply = 0.1 * LAB[pl.ds(r, n), :].astype(jnp.float32)
            new_u = u + diff_u * lap_u - react + rate * (1.0 - u) + supply
            new_v = v + diff_v * lap_v + react - (rate + kill) * v
            if halo:
                keep = halo_mask(p)
                new_u, new_v = new_u * keep, new_v * keep
            dst_u[p, pl.ds(r, n), :] = new_u
            dst_v[p, pl.ds(r, n), :] = new_v

        return body

    def first_tangent(p, r, n):
        shift = held(D, p, r, n)
        P1[p, pl.ds(r, n), :] = (1.0 - held(U0, p, r, n)) * shift
        Q1[p, pl.ds(r, n), :] = -held(V0, p, r, n) * shift

    def tangent(src_p, src_q, dst_p, dst_q, at_u, at_v, halo):
        def body(p, r, n):
            tan_p, lap_p = lap(src_p, p, r, n)
            tan_q, lap_q = lap(src_q, p, r, n)
            u, v = held(at_u, p, r, n), held(at_v, p, r, n)
            rate, shift = held(F, p, r, n), held(D, p, r, n)
            sq = v * v
            both = 2.0 * (u * v)
            new_p = tan_p + diff_u * lap_p - (sq + rate) * tan_p - both * tan_q + (1.0 - u) * shift
            new_q = tan_q + diff_v * lap_q + sq * tan_p + (both - rate - kill) * tan_q - v * shift
            if halo:
                keep = halo_mask(p)
                new_p, new_q = new_p * keep, new_q * keep
            dst_p[p, pl.ds(r, n), :] = new_p
            dst_q[p, pl.ds(r, n), :] = new_q

        return body

    def adjoint(src_a, src_b, at_u, at_v, p, r, n):
        a, lap_a = lap(src_a, p, r, n)
        b, lap_b = lap(src_b, p, r, n)
        u, v = held(at_u, p, r, n), held(at_v, p, r, n)
        rate = held(F, p, r, n)
        sq = v * v
        both = 2.0 * (u * v)
        new_a = a + diff_u * lap_a - (sq + rate) * a + sq * b
        new_b = b + diff_v * lap_b - both * a + (both - rate - kill) * b
        return a, b, u, v, new_a, new_b

    def second_adjoint(p, r, n):
        new_a, new_b = adjoint(A3, B3, U2, V2, p, r, n)[4:]
        A2[p, pl.ds(r, n), :] = new_a
        B2[p, pl.ds(r, n), :] = new_b

    def product(p, r, n):
        a, b, u, v, new_a, new_b = adjoint(A2, B2, U1, V1, p, r, n)
        total = (1.0 - held(U2, p, r, n)) * held(A3, p, r, n) - held(V2, p, r, n) * held(B3, p, r, n)
        total = total + (1.0 - u) * a - v * b
        total = total + (1.0 - held(U0, p, r, n)) * new_a - held(V0, p, r, n) * new_b
        G[p - LO, pl.ds(row(r - start), n), :] = total

    inner, ends, halos = (3, 1, 2), (2, 3, 2), (1, 5, 2)
    for copy in loads:
        copy.wait()
    for arrived in got_mate:
        arrived()
    sweep(inner, forward(U0, V0, U1, V1, False))

    for arrived in got_dir + got_feed:
        arrived()
    passed = []
    for side in (0, 1):
        planes = ((0, 2), (6, 8))[side]
        for step in range(1, exps):
            for ref in (
                D.at[planes[0] : planes[1], pl.ds(mine, part)],
                F.at[(1, 6)[side], pl.ds(mine, part)],
            ):
                passed.append(remote(ref, ref, peer(step=step), has[side], has[side]))
    for arrived in got_rows + passed:
        arrived()
    mate_row = row(start + edge_in)
    got_edges = [remote(
        D.at[:, pl.ds(mate_row, EDGE)], D.at[:, pl.ds(edge_out, EDGE)], peer(other=True))]
    for p in (1, 6):
        got_edges.append(remote(
            F.at[p, pl.ds(mate_row, EDGE)], F.at[p, pl.ds(edge_out, EDGE)], peer(other=True)))

    for arrived in got_one:
        arrived()
    sweep(ends, forward(U0, V0, U1, V1, False))
    sweep(inner, forward(U1, V1, U2, V2, False))
    for arrived in got_edges:
        arrived()
    sweep((1, 1, 6), first_tangent)
    sweep((2, 1, 4), tangent(P1, Q1, P2, Q2, U1, V1, False))
    sweep(inner, tangent(P2, Q2, A3, B3, U2, V2, False))

    pieces = [([], row(PAD + own * mate), EDGE)]
    pieces += [(got_two[k], row(start + top(k)), CHUNK) for k in range(blocks)]
    got_adj = []
    for waits, first, length in pieces:
        for arrived in waits:
            arrived()
        sweep((0, 7, 2), first_tangent, first, length)
        sweep(halos, forward(U0, V0, U1, V1, True), first, length)
        sweep(halos, tangent(P1, Q1, P2, Q2, U1, V1, True), first, length)
        sweep(ends, forward(U1, V1, U2, V2, False), first, length)
        sweep(ends, tangent(P2, Q2, A3, B3, U2, V2, False), first, length)
        got = []
        for side in (0, 1):
            for ref in (A3, B3):
                got.append(remote(
                    ref.at[(LO, HI)[side], pl.ds(first, length)],
                    ref.at[first_in[side], pl.ds(first, length)],
                    peer(side), has[side], has[1 - side]))
        got_adj.append(got)
    sweep(inner, second_adjoint)

    span = part // CHUNK
    base = count[0]
    count[0] += (exps - 1) * span
    got_add, leaving = [], []

    def finish(k):
        at = top(k)
        sweep((LO, 1, 4), product, row(start + at), CHUNK)
        for arrived in got_add[k]:
            arrived()
        for side in (0, 1):
            G[(0, 3)[side], pl.ds(at, CHUNK), :] += CN[side, pl.ds(at, CHUNK), :]
        step = lax.rem(at // part + exps - exp, exps)
        within = lax.rem(at, part)
        away = step > 0
        slot = jnp.maximum(step - 1, 0)
        i = base + slot * span + within // CHUNK
        copy = pltpu.make_async_remote_copy(
            src_ref=G.at[:, pl.ds(at, CHUNK)],
            dst_ref=R.at[slot, :, pl.ds(row(within), CHUNK)],
            send_sem=send.at[i], recv_sem=recv.at[i],
            device_id=peer(step=jnp.maximum(step, 1)), device_id_type=MESH,
        )
        pl.when(away)(copy.start)
        pending.append((away, copy))

    for k, (waits, first, length) in enumerate([(got_adj[0], *pieces[0][1:])] + [
        (got_adj[k + 1], *pieces[k + 1][1:]) for k in range(blocks)
    ]):
        for arrived in waits:
            arrived()
        sweep(ends, second_adjoint, first, length)
        if k == 0:
            continue
        at = top(k - 1)
        got = []
        for side in (0, 1):
            p, q = (LO, HI)[side], (1, 6)[side]
            C[side, pl.ds(at, CHUNK), :] = (
                (1.0 - held(U0, q, first, CHUNK)) * (diff_u * held(A2, p, first, CHUNK))
                - held(V0, q, first, CHUNK) * (diff_v * held(B2, p, first, CHUNK))
            )
            got.append(remote(
                C.at[side, pl.ds(at, CHUNK)], CN.at[1 - side, pl.ds(at, CHUNK)],
                peer(side), has[side], has[1 - side]))
        got_add.append(got)
        if k > 1:
            finish(k - 2)
    finish(blocks - 1)

    for step in range(1, exps):
        for m in range(span):
            rows_in = R.at[step - 1, :, pl.ds(m * CHUNK, CHUNK)]
            i = base + (step - 1) * span + m
            pltpu.make_async_copy(rows_in, rows_in, recv.at[i]).wait()
    kept = row(part * exp)
    for p in range(4):
        total = G[p, pl.ds(kept, part), :]
        for step in range(1, exps):
            total = total + R[step - 1, p]
        out[p] = total
    for sends, copy in pending:
        if sends is None:
            copy.wait_send()
        else:
            pl.when(sends)(copy.wait_send)


def solution(mesh):
    slabs, exps = mesh.shape["slab"], mesh.shape["exp"]

    def per_device(start_u, start_v, feed, labels, direction):
        planes, own, width = feed.shape
        part = own // exps
        tall = own + EDGE + 2 * PAD

        def field(*shape):
            return pltpu.VMEM(shape, jnp.float32)

        copies = 128 + 16 * exps
        return pl.pallas_call(
            functools.partial(kernel, slabs, exps),
            out_shape=jax.ShapeDtypeStruct((planes, part, width), jnp.float32),
            in_specs=[pl.BlockSpec(memory_space=pltpu.HBM)] * 5,
            out_specs=pl.BlockSpec(memory_space=pltpu.VMEM),
            scratch_shapes=(
                [field(8, tall, width)] * 4
                + [pltpu.VMEM((tall, width), jnp.int32)]
                + [field(8, tall, width)] * 12
                + [
                    field(2, own, width),
                    field(2, own, width),
                    field(planes, own, width),
                    field(exps - 1, planes, part, width),
                    pltpu.SemaphoreType.DMA((copies,)),
                    pltpu.SemaphoreType.DMA((copies,)),
                    pltpu.SemaphoreType.DMA((5,)),
                ]
            ),
            compiler_params=pltpu.CompilerParams(
                collective_id=0, has_side_effects=True, vmem_limit_bytes=62 * 1024 * 1024
            ),
        )(start_u[0], start_v[0], feed, labels[0], direction)

    placed = (
        P(("grp", "exp"), "slab", "sub", None),
        P(("grp", "exp"), "slab", "sub", None),
        P(("grp", "slab"), "sub", None),
        P(("grp", "exp"), "sub", None),
        P(("grp", "slab"), ("sub", "exp"), None),
    )
    return jax.shard_map(
        per_device,
        mesh=mesh,
        in_specs=placed,
        out_specs=P(("grp", "slab"), ("sub", "exp"), None),
        check_vma=False,
    )
```

```python
import functools

import jax
import jax.numpy as jnp
from jax import lax
from jax.experimental import pallas as pl
from jax.experimental.pallas import tpu as pltpu
from jax.sharding import PartitionSpec as P

diff_u = 0.15
diff_v = 0.075
kill = 0.06

EDGE = 8
PAD = 8
CHUNK = 32
BLOCK = 16
LO, HI = 2, 5
MESH = pl.DeviceIdType.MESH


def kernel(
    slabs, exps,
    u_in, v_in, feed_in, lab_in, dir_in, out,
    U0, V0, D, F, LAB, U1, V1, U2, V2, P1, Q1, P2, Q2, A3, B3, A2, B2,
    C, CN, G, R, send, recv, local,
):
    own, width = u_in.shape[1], u_in.shape[2]
    rows = own + EDGE
    part = own // exps
    grp, slab = lax.axis_index("grp"), lax.axis_index("slab")
    exp, sub = lax.axis_index("exp"), lax.axis_index("sub")
    has = (slab > 0, slab < slabs - 1)
    mate = 1 - sub

    def row(value):
        return pl.multiple_of(value, 8)

    start = row(PAD + EDGE * sub)
    edge_in = row((own - EDGE) * (1 - sub))
    edge_out = row(PAD + own * sub)
    mine = row(start + part * exp)

    def peer(side=None, step=0, other=False):
        z = slab if side is None else slab + (2 * side - 1)
        return (grp, z, lax.rem(exp + step, exps), mate if other else sub)

    count = [0]
    pending = []

    def remote(src, dst, target, sends=None, gets=None):
        i = count[0]
        count[0] += 1
        copy = pltpu.make_async_remote_copy(
            src_ref=src, dst_ref=dst, send_sem=send.at[i], recv_sem=recv.at[i],
            device_id=target, device_id_type=MESH,
        )
        if sends is None:
            copy.start()
        else:
            pl.when(sends)(copy.start)
        pending.append((sends, copy))

        def arrived():
            if gets is None:
                copy.wait_recv()
            else:
                pl.when(gets)(copy.wait_recv)

        return arrived

    loads = []
    for i, (src, dst) in enumerate([
        (u_in, U0.at[LO : HI + 1, pl.ds(start, own)]),
        (v_in, V0.at[LO : HI + 1, pl.ds(start, own)]),
        (feed_in, F.at[LO : HI + 1, pl.ds(start, own)]),
        (lab_in, LAB.at[pl.ds(start, own)]),
        (dir_in, D.at[LO : HI + 1, pl.ds(mine, part)]),
    ]):
        copy = pltpu.make_async_copy(src, dst, local.at[i])
        copy.start()
        loads.append(copy)

    barrier = pltpu.get_barrier_semaphore()

    def greet(target):
        pl.semaphore_signal(barrier, inc=1, device_id=target, device_id_type=MESH)

    greet(peer(other=True))
    for step in range(1, exps):
        greet(peer(step=step))
    for side in (0, 1):
        @pl.when(has[side])
        def _():
            greet(peer(side))
            greet(peer(side, other=True))

    for ref in (U0, V0, U1, V1, P1, Q1, P2, Q2, A3, B3, A2, B2):
        blank = jnp.zeros((ref.shape[0], PAD, width), jnp.float32)
        ref[:, :PAD, :] = blank
        ref[:, PAD + rows :, :] = blank
    for ref in (A2, B2):
        for p in (LO - 1, HI + 1):
            ref[p] = jnp.zeros(ref.shape[1:], jnp.float32)
    for side in (0, 1):
        @pl.when(jnp.logical_not(has[side]))
        def _():
            for ref in (U0, V0, D):
                for p in ((0, 1), (6, 7))[side]:
                    ref[p] = jnp.zeros(ref.shape[1:], jnp.float32)
            for ref in (F, A3, B3):
                ref[(1, 6)[side]] = jnp.zeros(ref.shape[1:], jnp.float32)
            CN[side] = jnp.zeros(CN.shape[1:], jnp.float32)

    near = jnp.where(has[0], 1, 0) + jnp.where(has[1], 1, 0)
    pl.semaphore_wait(barrier, exps + 2 * near)

    outer = (0, 3)
    second = (1, 2)
    first_in = (6, 1)
    second_in = (7, 0)
    pair = ((0, 2), (2, 4))
    pair_in = ((6, 8), (0, 2))

    got_dir, got_feed, got_one, got_two = [], [], [], []
    for side in (0, 1):
        a, b = pair[side]
        c, d = pair_in[side]
        got_dir.append(remote(
            dir_in.at[a:b], D.at[c:d, pl.ds(mine, part)], peer(side), has[side], has[1 - side]))
        got_feed.append(remote(
            feed_in.at[outer[side], pl.ds(row(part * exp), part)],
            F.at[first_in[side], pl.ds(mine, part)], peer(side), has[side], has[1 - side]))
    got_mate = []
    for src, dst in ((u_in, U0), (v_in, V0), (feed_in, F)):
        got_mate.append(remote(
            src.at[:, pl.ds(edge_in, EDGE)], dst.at[LO : HI + 1, pl.ds(edge_out, EDGE)],
            peer(other=True)))
    got_mate.append(remote(
        lab_in.at[pl.ds(edge_in, EDGE)], LAB.at[pl.ds(edge_out, EDGE)], peer(other=True)))
    got_rows = [
        remote(dir_in, D.at[LO : HI + 1, pl.ds(mine, part)], peer(step=step))
        for step in range(1, exps)
    ]
    for side in (0, 1):
        for src, dst in ((u_in, U0), (v_in, V0)):
            got_one.append(remote(
                src.at[outer[side]], dst.at[first_in[side], pl.ds(start, own)],
                peer(side), has[side], has[1 - side]))
    for side in (0, 1):
        a, b = pair[side]
        c, d = pair_in[side]
        for src, dst in ((u_in, U0), (v_in, V0)):
            got_one.append(remote(
                src.at[a:b, pl.ds(edge_in, EDGE)], dst.at[c:d, pl.ds(edge_out, EDGE)],
                peer(side, other=True), has[side], has[1 - side]))
    upward = 2 * exp >= exps
    blocks = own // CHUNK

    def top(k):
        return row(CHUNK * jnp.where(upward, k, blocks - 1 - k))

    for k in range(blocks):
        got = []
        for side in (0, 1):
            for src, dst in ((u_in, U0), (v_in, V0)):
                got.append(remote(
                    src.at[second[side], pl.ds(top(k), CHUNK)],
                    dst.at[second_in[side], pl.ds(row(start + top(k)), CHUNK)],
                    peer(side), has[side], has[1 - side]))
        got_two.append(got)

    def sweep(planes, body, first=PAD, length=rows):
        begin, stride, number = planes

        def plane(i, carry):
            p = begin + stride * i

            def block(j, inner):
                body(p, row(first + j * BLOCK), BLOCK)
                return inner

            lax.fori_loop(0, length // BLOCK, block, 0, unroll=True)
            if length % BLOCK:
                body(p, row(first + length // BLOCK * BLOCK), length % BLOCK)
            return carry

        lax.fori_loop(0, number, plane, 0, unroll=length <= CHUNK)

    def held(ref, p, r, n):
        return ref[p, pl.ds(r, n), :]

    def lap(ref, p, r, n):
        core = held(ref, p, r, n)
        wide = ref[p, pl.ds(row(r - 8), n + 16), :]
        lane = lax.broadcasted_iota(jnp.int32, core.shape, 1)
        total = held(ref, p + 1, r, n) + held(ref, p - 1, r, n)
        total = total + wide[9 : 9 + n] + wide[7 : 7 + n]
        total = total + jnp.where(lane == width - 1, 0.0, pltpu.roll(core, width - 1, 1))
        total = total + jnp.where(lane == 0, 0.0, pltpu.roll(core, 1, 1))
        return core, total - 6.0 * core

    def halo_mask(p):
        there = jnp.where(p < LO, has[0], jnp.where(p > HI, has[1], True))
        return jnp.where(there, 1.0, 0.0)

    def forward(src_u, src_v, dst_u, dst_v, halo):
        def body(p, r, n):
            u, lap_u = lap(src_u, p, r, n)
            v, lap_v = lap(src_v, p, r, n)
            rate = held(F, p, r, n)
            react = u * v * v
            supply = 0.1 * LAB[pl.ds(r, n), :].astype(jnp.float32)
            new_u = u + diff_u * lap_u - react + rate * (1.0 - u) + supply
            new_v = v + diff_v * lap_v + react - (rate + kill) * v
            if halo:
                keep = halo_mask(p)
                new_u, new_v = new_u * keep, new_v * keep
            dst_u[p, pl.ds(r, n), :] = new_u
            dst_v[p, pl.ds(r, n), :] = new_v

        return body

    def first_tangent(p, r, n):
        shift = held(D, p, r, n)
        P1[p, pl.ds(r, n), :] = (1.0 - held(U0, p, r, n)) * shift
        Q1[p, pl.ds(r, n), :] = -held(V0, p, r, n) * shift

    def tangent(src_p, src_q, dst_p, dst_q, at_u, at_v, halo):
        def body(p, r, n):
            tan_p, lap_p = lap(src_p, p, r, n)
            tan_q, lap_q = lap(src_q, p, r, n)
            u, v = held(at_u, p, r, n), held(at_v, p, r, n)
            rate, shift = held(F, p, r, n), held(D, p, r, n)
            sq = v * v
            both = 2.0 * (u * v)
            new_p = tan_p + diff_u * lap_p - (sq + rate) * tan_p - both * tan_q + (1.0 - u) * shift
            new_q = tan_q + diff_v * lap_q + sq * tan_p + (both - rate - kill) * tan_q - v * shift
            if halo:
                keep = halo_mask(p)
                new_p, new_q = new_p * keep, new_q * keep
            dst_p[p, pl.ds(r, n), :] = new_p
            dst_q[p, pl.ds(r, n), :] = new_q

        return body

    def adjoint(src_a, src_b, at_u, at_v, p, r, n):
        a, lap_a = lap(src_a, p, r, n)
        b, lap_b = lap(src_b, p, r, n)
        u, v = held(at_u, p, r, n), held(at_v, p, r, n)
        rate = held(F, p, r, n)
        sq = v * v
        both = 2.0 * (u * v)
        new_a = a + diff_u * lap_a - (sq + rate) * a + sq * b
        new_b = b + diff_v * lap_b - both * a + (both - rate - kill) * b
        return a, b, u, v, new_a, new_b

    def second_adjoint(p, r, n):
        new_a, new_b = adjoint(A3, B3, U2, V2, p, r, n)[4:]
        A2[p, pl.ds(r, n), :] = new_a
        B2[p, pl.ds(r, n), :] = new_b

    def product(p, r, n):
        a, b, u, v, new_a, new_b = adjoint(A2, B2, U1, V1, p, r, n)
        total = (1.0 - held(U2, p, r, n)) * held(A3, p, r, n) - held(V2, p, r, n) * held(B3, p, r, n)
        total = total + (1.0 - u) * a - v * b
        total = total + (1.0 - held(U0, p, r, n)) * new_a - held(V0, p, r, n) * new_b
        G[p - LO, pl.ds(row(r - start), n), :] = total

    inner, ends, halos = (3, 1, 2), (2, 3, 2), (1, 5, 2)
    for copy in loads:
        copy.wait()
    for arrived in got_mate:
        arrived()
    sweep(inner, forward(U0, V0, U1, V1, False))

    for arrived in got_dir + got_feed:
        arrived()
    passed = []
    for side in (0, 1):
        planes = ((0, 2), (6, 8))[side]
        for step in range(1, exps):
            for ref in (
                D.at[planes[0] : planes[1], pl.ds(mine, part)],
                F.at[(1, 6)[side], pl.ds(mine, part)],
            ):
                passed.append(remote(ref, ref, peer(step=step), has[side], has[side]))
    for arrived in got_rows + passed:
        arrived()
    mate_row = row(start + edge_in)
    got_edges = [remote(
        D.at[:, pl.ds(mate_row, EDGE)], D.at[:, pl.ds(edge_out, EDGE)], peer(other=True))]
    for p in (1, 6):
        got_edges.append(remote(
            F.at[p, pl.ds(mate_row, EDGE)], F.at[p, pl.ds(edge_out, EDGE)], peer(other=True)))

    for arrived in got_one:
        arrived()
    sweep(ends, forward(U0, V0, U1, V1, False))
    sweep(inner, forward(U1, V1, U2, V2, False))
    for arrived in got_edges:
        arrived()
    sweep((1, 1, 6), first_tangent)
    sweep((2, 1, 4), tangent(P1, Q1, P2, Q2, U1, V1, False))
    sweep(inner, tangent(P2, Q2, A3, B3, U2, V2, False))

    pieces = [([], row(PAD + own * mate), EDGE)]
    pieces += [(got_two[k], row(start + top(k)), CHUNK) for k in range(blocks)]
    got_adj = []
    for waits, first, length in pieces:
        for arrived in waits:
            arrived()
        sweep((0, 7, 2), first_tangent, first, length)
        sweep(halos, forward(U0, V0, U1, V1, True), first, length)
        sweep(halos, tangent(P1, Q1, P2, Q2, U1, V1, True), first, length)
        sweep(ends, forward(U1, V1, U2, V2, False), first, length)
        sweep(ends, tangent(P2, Q2, A3, B3, U2, V2, False), first, length)
        got = []
        for side in (0, 1):
            for ref in (A3, B3):
                got.append(remote(
                    ref.at[(LO, HI)[side], pl.ds(first, length)],
                    ref.at[first_in[side], pl.ds(first, length)],
                    peer(side), has[side], has[1 - side]))
        got_adj.append(got)
    sweep(inner, second_adjoint)

    span = part // CHUNK
    base = count[0]
    count[0] += (exps - 1) * span
    got_add, leaving = [], []

    def finish(k):
        at = top(k)
        sweep((LO, 1, 4), product, row(start + at), CHUNK)
        for arrived in got_add[k]:
            arrived()
        for side in (0, 1):
            G[(0, 3)[side], pl.ds(at, CHUNK), :] += CN[side, pl.ds(at, CHUNK), :]
        step = lax.rem(at // part + exps - exp, exps)
        within = lax.rem(at, part)
        away = step > 0
        slot = jnp.maximum(step - 1, 0)
        i = base + slot * span + within // CHUNK
        copy = pltpu.make_async_remote_copy(
            src_ref=G.at[:, pl.ds(at, CHUNK)],
            dst_ref=R.at[slot, :, pl.ds(row(within), CHUNK)],
            send_sem=send.at[i], recv_sem=recv.at[i],
            device_id=peer(step=jnp.maximum(step, 1)), device_id_type=MESH,
        )
        pl.when(away)(copy.start)
        pending.append((away, copy))

    for k, (waits, first, length) in enumerate([(got_adj[0], *pieces[0][1:])] + [
        (got_adj[k + 1], *pieces[k + 1][1:]) for k in range(blocks)
    ]):
        for arrived in waits:
            arrived()
        sweep(ends, second_adjoint, first, length)
        if k == 0:
            continue
        at = top(k - 1)
        got = []
        for side in (0, 1):
            p, q = (LO, HI)[side], (1, 6)[side]
            C[side, pl.ds(at, CHUNK), :] = (
                (1.0 - held(U0, q, first, CHUNK)) * (diff_u * held(A2, p, first, CHUNK))
                - held(V0, q, first, CHUNK) * (diff_v * held(B2, p, first, CHUNK))
            )
            got.append(remote(
                C.at[side, pl.ds(at, CHUNK)], CN.at[1 - side, pl.ds(at, CHUNK)],
                peer(side), has[side], has[1 - side]))
        got_add.append(got)
        if k > 1:
            finish(k - 2)
    finish(blocks - 1)

    for step in range(1, exps):
        for m in range(span):
            rows_in = R.at[step - 1, :, pl.ds(m * CHUNK, CHUNK)]
            i = base + (step - 1) * span + m
            pltpu.make_async_copy(rows_in, rows_in, recv.at[i]).wait()
    kept = row(part * exp)
    for p in range(4):
        total = G[p, pl.ds(kept, part), :]
        for step in range(1, exps):
            total = total + R[step - 1, p]
        out[p] = total
    for sends, copy in pending:
        if sends is None:
            copy.wait_send()
        else:
            pl.when(sends)(copy.wait_send)


def solution(mesh):
    slabs, exps = mesh.shape["slab"], mesh.shape["exp"]

    def per_device(start_u, start_v, feed, labels, direction):
        planes, own, width = feed.shape
        part = own // exps
        tall = own + EDGE + 2 * PAD

        def field(*shape):
            return pltpu.VMEM(shape, jnp.float32)

        copies = 128 + 16 * exps
        return pl.pallas_call(
            functools.partial(kernel, slabs, exps),
            out_shape=jax.ShapeDtypeStruct((planes, part, width), jnp.float32),
            in_specs=[pl.BlockSpec(memory_space=pltpu.HBM)] * 5,
            out_specs=pl.BlockSpec(memory_space=pltpu.VMEM),
            scratch_shapes=(
                [field(8, tall, width)] * 4
                + [pltpu.VMEM((tall, width), jnp.int32)]
                + [field(8, tall, width)] * 12
                + [
                    field(2, own, width),
                    field(2, own, width),
                    field(planes, own, width),
                    field(exps - 1, planes, part, width),
                    pltpu.SemaphoreType.DMA((copies,)),
                    pltpu.SemaphoreType.DMA((copies,)),
                    pltpu.SemaphoreType.DMA((5,)),
                ]
            ),
            compiler_params=pltpu.CompilerParams(
                collective_id=0, has_side_effects=True, vmem_limit_bytes=62 * 1024 * 1024
            ),
        )(start_u[0], start_v[0], feed, labels[0], direction)

    placed = (
        P(("grp", "exp"), "slab", "sub", None),
        P(("grp", "exp"), "slab", "sub", None),
        P(("grp", "slab"), "sub", None),
        P(("grp", "exp"), "sub", None),
        P(("grp", "slab"), ("sub", "exp"), None),
    )
    return jax.shard_map(
        per_device,
        mesh=mesh,
        in_specs=placed,
        out_specs=P(("grp", "slab"), ("sub", "exp"), None),
        check_vma=False,
    )
```

```python
import functools

import jax
import jax.numpy as jnp
from jax import lax
from jax.experimental import pallas as pl
from jax.experimental.pallas import tpu as pltpu
from jax.sharding import PartitionSpec as P

diff_u = 0.15
diff_v = 0.075
kill = 0.06

EDGE = 8
PAD = 8
CHUNK = 32
BLOCK = 16
LO, HI = 2, 5
MESH = pl.DeviceIdType.MESH


def kernel(
    slabs, exps,
    u_in, v_in, feed_in, lab_in, dir_in, out,
    U0, V0, D, F, LAB, U1, V1, U2, V2, P1, Q1, P2, Q2, AB, A2, B2,
    C, CN, G, R, send, recv, local,
):
    own, width = u_in.shape[1], u_in.shape[2]
    rows = own + EDGE
    A3, B3 = AB.at[0], AB.at[1]
    part = own // exps
    grp, slab = lax.axis_index("grp"), lax.axis_index("slab")
    exp, sub = lax.axis_index("exp"), lax.axis_index("sub")
    has = (slab > 0, slab < slabs - 1)
    mate = 1 - sub

    def row(value):
        return pl.multiple_of(value, 8)

    start = row(PAD + EDGE * sub)
    edge_in = row((own - EDGE) * (1 - sub))
    edge_out = row(PAD + own * sub)
    mine = row(start + part * exp)

    def peer(side=None, step=0, other=False):
        z = slab if side is None else slab + (2 * side - 1)
        return (grp, z, lax.rem(exp + step, exps), mate if other else sub)

    count = [0]
    pending = []

    def remote(src, dst, target, sends=None, gets=None):
        i = count[0]
        count[0] += 1
        copy = pltpu.make_async_remote_copy(
            src_ref=src, dst_ref=dst, send_sem=send.at[i], recv_sem=recv.at[i],
            device_id=target, device_id_type=MESH,
        )
        if sends is None:
            copy.start()
        else:
            pl.when(sends)(copy.start)
        pending.append((sends, copy))

        def arrived():
            if gets is None:
                copy.wait_recv()
            else:
                pl.when(gets)(copy.wait_recv)

        return arrived

    barrier = pltpu.get_barrier_semaphore()

    def greet(target):
        pl.semaphore_signal(barrier, inc=1, device_id=target, device_id_type=MESH)

    greet(peer(other=True))
    for step in range(1, exps):
        greet(peer(step=step))
    for side in (0, 1):
        @pl.when(has[side])
        def _():
            greet(peer(side))
            greet(peer(side, other=True))

    loads = []
    for i, (src, dst) in enumerate([
        (u_in, U0.at[LO : HI + 1, pl.ds(start, own)]),
        (v_in, V0.at[LO : HI + 1, pl.ds(start, own)]),
        (feed_in, F.at[LO : HI + 1, pl.ds(start, own)]),
        (lab_in, LAB.at[pl.ds(start, own)]),
        (dir_in, D.at[LO : HI + 1, pl.ds(mine, part)]),
    ]):
        copy = pltpu.make_async_copy(src, dst, local.at[i])
        copy.start()
        loads.append(copy)

    for ref in (U0, V0, U1, V1, P1, Q1, P2, Q2, A3, B3, A2, B2):
        blank = jnp.zeros((ref.shape[0], PAD, width), jnp.float32)
        ref[:, :PAD, :] = blank
        ref[:, PAD + rows :, :] = blank
    for ref in (A2, B2):
        for p in (LO - 1, HI + 1):
            ref[p] = jnp.zeros(ref.shape[1:], jnp.float32)
    for side in (0, 1):
        @pl.when(jnp.logical_not(has[side]))
        def _():
            for ref in (U0, V0, D):
                for p in ((0, 1), (6, 7))[side]:
                    ref[p] = jnp.zeros(ref.shape[1:], jnp.float32)
            for ref in (F, A3, B3):
                ref[(1, 6)[side]] = jnp.zeros(ref.shape[1:], jnp.float32)
            CN[side] = jnp.zeros(CN.shape[1:], jnp.float32)

    near = jnp.where(has[0], 1, 0) + jnp.where(has[1], 1, 0)
    pl.semaphore_wait(barrier, exps + 2 * near)

    outer = (0, 3)
    second = (1, 2)
    first_in = (6, 1)
    second_in = (7, 0)
    pair = ((0, 2), (2, 4))
    pair_in = ((6, 8), (0, 2))

    got_dir, got_feed, got_one, got_two = [], [], [], []
    for side in (0, 1):
        a, b = pair[side]
        c, d = pair_in[side]
        got_dir.append(remote(
            dir_in.at[a:b], D.at[c:d, pl.ds(mine, part)], peer(side), has[side], has[1 - side]))
        got_feed.append(remote(
            feed_in.at[outer[side], pl.ds(row(part * exp), part)],
            F.at[first_in[side], pl.ds(mine, part)], peer(side), has[side], has[1 - side]))
    got_mate = []
    for src, dst in ((u_in, U0), (v_in, V0), (feed_in, F)):
        got_mate.append(remote(
            src.at[:, pl.ds(edge_in, EDGE)], dst.at[LO : HI + 1, pl.ds(edge_out, EDGE)],
            peer(other=True)))
    got_mate.append(remote(
        lab_in.at[pl.ds(edge_in, EDGE)], LAB.at[pl.ds(edge_out, EDGE)], peer(other=True)))
    got_rows = [
        remote(dir_in, D.at[LO : HI + 1, pl.ds(mine, part)], peer(step=step))
        for step in range(1, exps)
    ]
    for side in (0, 1):
        for src, dst in ((u_in, U0), (v_in, V0)):
            got_one.append(remote(
                src.at[outer[side]], dst.at[first_in[side], pl.ds(start, own)],
                peer(side), has[side], has[1 - side]))
    for side in (0, 1):
        a, b = pair[side]
        c, d = pair_in[side]
        for src, dst in ((u_in, U0), (v_in, V0)):
            got_one.append(remote(
                src.at[a:b, pl.ds(edge_in, EDGE)], dst.at[c:d, pl.ds(edge_out, EDGE)],
                peer(side, other=True), has[side], has[1 - side]))
    upward = 2 * exp >= exps
    blocks = own // CHUNK

    def top(k):
        return row(CHUNK * jnp.where(upward, k, blocks - 1 - k))

    for k in range(blocks):
        got = []
        for side in (0, 1):
            for src, dst in ((u_in, U0), (v_in, V0)):
                got.append(remote(
                    src.at[second[side], pl.ds(top(k), CHUNK)],
                    dst.at[second_in[side], pl.ds(row(start + top(k)), CHUNK)],
                    peer(side), has[side], has[1 - side]))
        got_two.append(got)

    def sweep(planes, body, first=PAD, length=rows):
        begin, stride, number = planes

        def plane(i, carry):
            p = begin + stride * i

            def block(j, inner):
                body(p, row(first + j * BLOCK), BLOCK)
                return inner

            lax.fori_loop(0, length // BLOCK, block, 0, unroll=True)
            if length % BLOCK:
                body(p, row(first + length // BLOCK * BLOCK), length % BLOCK)
            return carry

        lax.fori_loop(0, number, plane, 0, unroll=length <= CHUNK)

    def held(ref, p, r, n):
        return ref[p, pl.ds(r, n), :]

    def lap(ref, p, r, n):
        core = held(ref, p, r, n)
        wide = ref[p, pl.ds(row(r - 8), n + 16), :]
        lane = lax.broadcasted_iota(jnp.int32, core.shape, 1)
        total = held(ref, p + 1, r, n) + held(ref, p - 1, r, n)
        total = total + wide[9 : 9 + n] + wide[7 : 7 + n]
        total = total + jnp.where(lane == width - 1, 0.0, pltpu.roll(core, width - 1, 1))
        total = total + jnp.where(lane == 0, 0.0, pltpu.roll(core, 1, 1))
        return core, total - 6.0 * core

    def halo_mask(p):
        there = jnp.where(p < LO, has[0], jnp.where(p > HI, has[1], True))
        return jnp.where(there, 1.0, 0.0)

    def forward(src_u, src_v, dst_u, dst_v, halo):
        def body(p, r, n):
            u, lap_u = lap(src_u, p, r, n)
            v, lap_v = lap(src_v, p, r, n)
            rate = held(F, p, r, n)
            react = u * v * v
            supply = 0.1 * LAB[pl.ds(r, n), :].astype(jnp.float32)
            new_u = u + diff_u * lap_u - react + rate * (1.0 - u) + supply
            new_v = v + diff_v * lap_v + react - (rate + kill) * v
            if halo:
                keep = halo_mask(p)
                new_u, new_v = new_u * keep, new_v * keep
            dst_u[p, pl.ds(r, n), :] = new_u
            dst_v[p, pl.ds(r, n), :] = new_v

        return body

    def first_tangent(p, r, n):
        shift = held(D, p, r, n)
        P1[p, pl.ds(r, n), :] = (1.0 - held(U0, p, r, n)) * shift
        Q1[p, pl.ds(r, n), :] = -held(V0, p, r, n) * shift

    def tangent(src_p, src_q, dst_p, dst_q, at_u, at_v, halo):
        def body(p, r, n):
            tan_p, lap_p = lap(src_p, p, r, n)
            tan_q, lap_q = lap(src_q, p, r, n)
            u, v = held(at_u, p, r, n), held(at_v, p, r, n)
            rate, shift = held(F, p, r, n), held(D, p, r, n)
            sq = v * v
            both = 2.0 * (u * v)
            new_p = tan_p + diff_u * lap_p - (sq + rate) * tan_p - both * tan_q + (1.0 - u) * shift
            new_q = tan_q + diff_v * lap_q + sq * tan_p + (both - rate - kill) * tan_q - v * shift
            if halo:
                keep = halo_mask(p)
                new_p, new_q = new_p * keep, new_q * keep
            dst_p[p, pl.ds(r, n), :] = new_p
            dst_q[p, pl.ds(r, n), :] = new_q

        return body

    def adjoint(src_a, src_b, at_u, at_v, p, r, n):
        a, lap_a = lap(src_a, p, r, n)
        b, lap_b = lap(src_b, p, r, n)
        u, v = held(at_u, p, r, n), held(at_v, p, r, n)
        rate = held(F, p, r, n)
        sq = v * v
        both = 2.0 * (u * v)
        new_a = a + diff_u * lap_a - (sq + rate) * a + sq * b
        new_b = b + diff_v * lap_b - both * a + (both - rate - kill) * b
        return a, b, u, v, new_a, new_b

    def second_adjoint(p, r, n):
        new_a, new_b = adjoint(A3, B3, U2, V2, p, r, n)[4:]
        A2[p, pl.ds(r, n), :] = new_a
        B2[p, pl.ds(r, n), :] = new_b

    def product(p, r, n):
        a, b, u, v, new_a, new_b = adjoint(A2, B2, U1, V1, p, r, n)
        total = (1.0 - held(U2, p, r, n)) * held(A3, p, r, n) - held(V2, p, r, n) * held(B3, p, r, n)
        total = total + (1.0 - u) * a - v * b
        total = total + (1.0 - held(U0, p, r, n)) * new_a - held(V0, p, r, n) * new_b
        G[p - LO, pl.ds(row(r - start), n), :] = total

    inner, ends, halos = (3, 1, 2), (2, 3, 2), (1, 5, 2)
    for copy in loads:
        copy.wait()
    for arrived in got_mate:
        arrived()
    sweep(inner, forward(U0, V0, U1, V1, False))

    for arrived in got_dir + got_feed:
        arrived()
    passed = []
    for side in (0, 1):
        planes = ((0, 2), (6, 8))[side]
        for step in range(1, exps):
            for ref in (
                D.at[planes[0] : planes[1], pl.ds(mine, part)],
                F.at[(1, 6)[side], pl.ds(mine, part)],
            ):
                passed.append(remote(ref, ref, peer(step=step), has[side], has[side]))
    for arrived in got_rows + passed:
        arrived()
    mate_row = row(start + edge_in)
    got_edges = [remote(
        D.at[:, pl.ds(mate_row, EDGE)], D.at[:, pl.ds(edge_out, EDGE)], peer(other=True))]
    for p in (1, 6):
        got_edges.append(remote(
            F.at[p, pl.ds(mate_row, EDGE)], F.at[p, pl.ds(edge_out, EDGE)], peer(other=True)))

    for arrived in got_one:
        arrived()
    sweep(ends, forward(U0, V0, U1, V1, False))
    sweep(inner, forward(U1, V1, U2, V2, False))
    for arrived in got_edges:
        arrived()
    sweep((1, 1, 6), first_tangent)
    sweep((2, 1, 4), tangent(P1, Q1, P2, Q2, U1, V1, False))
    sweep(inner, tangent(P2, Q2, A3, B3, U2, V2, False))

    pieces = [([], row(PAD + own * mate), EDGE)]
    pieces += [(got_two[k], row(start + top(k)), CHUNK) for k in range(blocks)]
    got_adj = []
    for waits, first, length in pieces:
        for arrived in waits:
            arrived()
        sweep((0, 7, 2), first_tangent, first, length)
        sweep(halos, forward(U0, V0, U1, V1, True), first, length)
        sweep(halos, tangent(P1, Q1, P2, Q2, U1, V1, True), first, length)
        sweep(ends, forward(U1, V1, U2, V2, False), first, length)
        sweep(ends, tangent(P2, Q2, A3, B3, U2, V2, False), first, length)
        got = []
        for side in (0, 1):
            got.append(remote(
                AB.at[:, (LO, HI)[side], pl.ds(first, length)],
                AB.at[:, first_in[side], pl.ds(first, length)],
                peer(side), has[side], has[1 - side]))
        got_adj.append(got)
    sweep(inner, second_adjoint)

    span = part // CHUNK
    base = count[0]
    count[0] += (exps - 1) * span
    got_add, leaving = [], []

    def finish(k):
        at = top(k)
        sweep((LO, 1, 4), product, row(start + at), CHUNK)
        for arrived in got_add[k]:
            arrived()
        for side in (0, 1):
            G[(0, 3)[side], pl.ds(at, CHUNK), :] += CN[side, pl.ds(at, CHUNK), :]
        step = lax.rem(at // part + exps - exp, exps)
        within = lax.rem(at, part)
        away = step > 0
        slot = jnp.maximum(step - 1, 0)
        i = base + slot * span + within // CHUNK
        copy = pltpu.make_async_remote_copy(
            src_ref=G.at[:, pl.ds(at, CHUNK)],
            dst_ref=R.at[slot, :, pl.ds(row(within), CHUNK)],
            send_sem=send.at[i], recv_sem=recv.at[i],
            device_id=peer(step=jnp.maximum(step, 1)), device_id_type=MESH,
        )
        pl.when(away)(copy.start)
        pending.append((away, copy))

    for k, (waits, first, length) in enumerate([(got_adj[0], *pieces[0][1:])] + [
        (got_adj[k + 1], *pieces[k + 1][1:]) for k in range(blocks)
    ]):
        for arrived in waits:
            arrived()
        sweep(ends, second_adjoint, first, length)
        if k == 0:
            continue
        at = top(k - 1)
        got = []
        for side in (0, 1):
            p, q = (LO, HI)[side], (1, 6)[side]
            C[side, pl.ds(at, CHUNK), :] = (
                (1.0 - held(U0, q, first, CHUNK)) * (diff_u * held(A2, p, first, CHUNK))
                - held(V0, q, first, CHUNK) * (diff_v * held(B2, p, first, CHUNK))
            )
            got.append(remote(
                C.at[side, pl.ds(at, CHUNK)], CN.at[1 - side, pl.ds(at, CHUNK)],
                peer(side), has[side], has[1 - side]))
        got_add.append(got)
        if k > 1:
            finish(k - 2)
    finish(blocks - 1)

    for step in range(1, exps):
        for m in range(span):
            rows_in = R.at[step - 1, :, pl.ds(m * CHUNK, CHUNK)]
            i = base + (step - 1) * span + m
            pltpu.make_async_copy(rows_in, rows_in, recv.at[i]).wait()
    kept = row(part * exp)
    for p in range(4):
        total = G[p, pl.ds(kept, part), :]
        for step in range(1, exps):
            total = total + R[step - 1, p]
        out[p] = total
    for sends, copy in pending:
        if sends is None:
            copy.wait_send()
        else:
            pl.when(sends)(copy.wait_send)


def solution(mesh):
    slabs, exps = mesh.shape["slab"], mesh.shape["exp"]

    def per_device(start_u, start_v, feed, labels, direction):
        planes, own, width = feed.shape
        part = own // exps
        tall = own + EDGE + 2 * PAD

        def field(*shape):
            return pltpu.VMEM(shape, jnp.float32)

        copies = 128 + 16 * exps
        return pl.pallas_call(
            functools.partial(kernel, slabs, exps),
            out_shape=jax.ShapeDtypeStruct((planes, part, width), jnp.float32),
            in_specs=[pl.BlockSpec(memory_space=pltpu.HBM)] * 5,
            out_specs=pl.BlockSpec(memory_space=pltpu.VMEM),
            scratch_shapes=(
                [field(8, tall, width)] * 4
                + [pltpu.VMEM((tall, width), jnp.int32)]
                + [field(8, tall, width)] * 8
                + [field(2, 8, tall, width)]
                + [field(8, tall, width)] * 2
                + [
                    field(2, own, width),
                    field(2, own, width),
                    field(planes, own, width),
                    field(exps - 1, planes, part, width),
                    pltpu.SemaphoreType.DMA((copies,)),
                    pltpu.SemaphoreType.DMA((copies,)),
                    pltpu.SemaphoreType.DMA((5,)),
                ]
            ),
            compiler_params=pltpu.CompilerParams(
                collective_id=0, has_side_effects=True, vmem_limit_bytes=62 * 1024 * 1024
            ),
        )(start_u[0], start_v[0], feed, labels[0], direction)

    placed = (
        P(("grp", "exp"), "slab", "sub", None),
        P(("grp", "exp"), "slab", "sub", None),
        P(("grp", "slab"), "sub", None),
        P(("grp", "exp"), "sub", None),
        P(("grp", "slab"), ("sub", "exp"), None),
    )
    return jax.shard_map(
        per_device,
        mesh=mesh,
        in_specs=placed,
        out_specs=P(("grp", "slab"), ("sub", "exp"), None),
        check_vma=False,
    )
```
